256 devices in a mesh: ta: 4 (over x), col: 4 (over z_hi), vert: 16 (over y, z_lo, core).
Axes of the slice: x: 4, y: 4, z: 8 (z_hi: 4, z_lo: 2; z = z_hi * 2 + z_lo), core: 2. Of those that a mesh axis runs over, the one named last changes fastest.
Arguments:
- voltages: bfloat16 [4096, 262144], P(('vert', 'col'), 'ta'), may hold values from -6 to 6
- taps: float32 [4, 16384], replicated, may hold values from -3 to 3
- channels: int32 [16], replicated, may hold values from 0 to 8191
Outputs:
- visibilities: bfloat16 [16, 2, 4096, 4096], P('col', None, 'vert', 'ta')
The draws below stay inside these ranges and needn't reach their ends.
Inputs may be any that keep to these rules, and one draw needn't show every extreme that they name: `channels`: channel numbers of the subset, possibly repeated.
All inputs are finite; a program needn't handle non-finite values.
Results may differ from the reference program's by a relative error of at most 0.0057.
Values may be sent and summed in bfloat16 or wider, within the bound.
No kernel may reach another device: no remote copies, remote signals or barrier semaphores. Data moves between devices by JAX's collectives and lax.ppermute only.
A program may use at most 192 MiB of HBM per device.

```python
import math
import jax
import jax.numpy as jnp
from jax import lax

NI = 4096
FRAME = 16384
TAPS = 4
CHAN = 16
SPECTRA = 16
SAMPLES = 262144


def set_ends(drawn, key, low, largest):
    extent = drawn.shape
    spot = [jax.random.randint(jax.random.fold_in(key, axis), (), 0, extent[axis]) for axis in range(len(extent))]
    drawn = drawn.at[tuple(spot)].set(low)
    longest = extent.index(max(extent))
    spot[longest] = (spot[longest] + 1) % extent[longest]
    return drawn.at[tuple(spot)].set(largest)


def block_levels(stream_key, extent, split, least, largest):
    level = 1.0
    for dim, parts in split:
        draws = jax.random.uniform(jax.random.fold_in(jax.random.fold_in(stream_key, 6), dim), (parts,), jnp.float32, least / len(split), largest / len(split))
        level = level * jnp.repeat(jnp.exp(draws), extent[dim] // parts).reshape((-1,) + (1,) * (len(extent) - 1 - dim))
    return level


def scatter_about(stream_key, dims, deviation, bound, split=(), dtype=jnp.bfloat16):
    factor_of = block_levels(stream_key, dims, split, -0.22, 0.18) if split else 1.0
    result = jax.random.normal(stream_key, dims, jnp.float32) * deviation * factor_of
    return jnp.minimum(jnp.maximum(result, -bound), bound).astype(dtype)


def setup_inputs(seed: int = 0) -> dict:
    keys = jax.random.split(jax.random.key(seed), 4)
    return {
        "voltages": scatter_about(keys[0], (NI, SAMPLES), 1.0, 6.0, ((0, 64), (1, 4))),
        "taps": scatter_about(keys[1], (TAPS, FRAME), 0.5, 3.0, (), jnp.float32),
        "channels": set_ends(jax.random.randint(keys[2], (CHAN,), 0, FRAME // 2), jax.random.fold_in(keys[2], 1), 0, (FRAME // 2) - 1).astype(jnp.int32),
    }


def dft_table(channels, length):
    index = lax.broadcasted_iota(jnp.int32, (length, channels.shape[0]), 0)
    phase = index * channels[None, :].astype(jnp.int32) % length
    angle = phase.astype(jnp.float32) * (2.0 * math.pi / length)
    scale = 1.0 / math.sqrt(length)
    return jnp.concatenate([jnp.cos(angle), -jnp.sin(angle)], axis=1) * scale

def reference(voltages, taps, channels):
    groups = math.gcd(NI, 64)
    table = dft_table(channels, FRAME)
    frames = voltages.reshape(groups, NI // groups, SPECTRA, FRAME)

    def filter_group(block):
        padded = jnp.concatenate([jnp.zeros((block.shape[0], TAPS - 1, FRAME), jnp.bfloat16), block], axis=1)
        filtered = jnp.zeros((block.shape[0], SPECTRA, FRAME), jnp.float32)
        for tap in range(TAPS):
            filtered = filtered + taps[tap][None, None, :] * padded[:, tap:tap + SPECTRA].astype(jnp.float32)
        spec = jnp.dot(filtered.reshape(-1, FRAME), table, precision=lax.Precision.HIGHEST, preferred_element_type=jnp.float32)
        return spec.reshape(block.shape[0], SPECTRA, 2 * CHAN).astype(jnp.bfloat16)
    spectra = lax.map(filter_group, frames).reshape(NI, SPECTRA, 2 * CHAN)
    real_parts = jnp.transpose(spectra[:, :, :CHAN], (2, 1, 0))
    imag_parts = jnp.transpose(spectra[:, :, CHAN:], (2, 1, 0))

    def correlate(pair):
        real_part, imag_part = pair
        left = jnp.concatenate([real_part, imag_part], axis=0)
        right_real = jnp.concatenate([real_part, imag_part], axis=0)
        right_imag = jnp.concatenate([-imag_part, real_part], axis=0)
        right = jnp.concatenate([right_real, right_imag], axis=1)
        product = jnp.dot(left.T, right, preferred_element_type=jnp.float32) * (1.0 / SPECTRA)
        product = product.reshape(NI, 2, NI)
        return jnp.transpose(product, (1, 0, 2)).astype(jnp.bfloat16)
    return lax.map(correlate, (real_parts, imag_parts))
```

```python
import functools
import math

import jax
import jax.numpy as jnp
from jax import lax
from jax.experimental import pallas as pl
from jax.experimental.pallas import tpu as pltpu
from jax.sharding import Mesh, PartitionSpec as P

FRAMES = 4
TAPS = 4
CHUNK = 2048
LANES = 128
ROWS = 32
HALF = 64


def row_channels(chan_ref, shape):
    row = lax.broadcasted_iota(jnp.int32, shape, 0)
    which = row // 8 * 4 + row % 4
    chan = jnp.zeros(shape, jnp.int32)
    for c in range(16):
        chan = jnp.where(which == c, chan_ref[c], chan)
    return chan, row // 4 % 2


def filterbank_kernel(chan_ref, v0, v1, v2, v3, taps_ref, own_ref, next_ref, cos_ref, sin_ref, chan_tab, acc_ref):
    step = pl.program_id(0)
    length = pl.num_programs(0) * CHUNK
    turn = 2.0 * math.pi / length
    mask = length - 1

    @pl.when(step == 0)
    def _():
        chan, _ = row_channels(chan_ref, (ROWS, LANES))
        chan_tab[...] = chan
        lane = lax.broadcasted_iota(jnp.int32, (ROWS, LANES), 1)
        fine = ((lane * chan) & mask).astype(jnp.float32) * turn
        fine_cos, fine_sin = jnp.cos(fine), jnp.sin(fine)
        coarse = ((lane * LANES * chan) & mask).astype(jnp.float32) * turn
        coarse_cos, coarse_sin = jnp.cos(coarse), jnp.sin(coarse)
        for u in range(CHUNK // LANES):
            at = slice(u * LANES, (u + 1) * LANES)
            cu, su = coarse_cos[:, u : u + 1], coarse_sin[:, u : u + 1]
            cos_ref[:, at] = cu * fine_cos - su * fine_sin
            sin_ref[:, at] = su * fine_cos + cu * fine_sin

    part = lax.broadcasted_iota(jnp.int32, (ROWS, LANES), 0) // 4 % 2
    base = ((chan_tab[...] * (step * CHUNK) + part * (length // 4)) & mask).astype(jnp.float32) * turn
    scale = 1.0 / math.sqrt(length)
    base_cos = (jnp.cos(base) * scale)[:, :1]
    base_sin = (jnp.sin(base) * scale)[:, :1]
    table = base_cos * cos_ref[...] - base_sin * sin_ref[...]
    high, low = [], []
    for t in range(TAPS):
        w = table * taps_ref[t : t + 1, :]
        h = w.astype(jnp.bfloat16)
        high.append(h)
        low.append((w - h.astype(jnp.float32)).astype(jnp.bfloat16))
    weights = jnp.concatenate(high + low, axis=0)
    frames = jnp.concatenate([v0[...], v1[...], v2[...], v3[...]], axis=0)
    prod = lax.dot_general(
        weights, frames, (((1,), (1,)), ((), ())), preferred_element_type=jnp.float32
    )
    acc_ref[...] = jnp.where(step == 0, 0.0, acc_ref[...]) + prod

    @pl.when(step == pl.num_programs(0) - 1)
    def _():
        g = acc_ref[: TAPS * ROWS] + acc_ref[TAPS * ROWS :]

        def term(t, f):
            return g[t * ROWS : (t + 1) * ROWS, f * HALF : (f + 1) * HALF]

        own, after = [], []
        for s in range(FRAMES):
            own.append(sum(term(f - s + 3, f) for f in range(s + 1)))
            if s < TAPS - 1:
                after.append(sum(term(f - 1 - s, f) for f in range(s + 1, FRAMES)))
        after.append(jnp.zeros_like(after[0]))
        own_ref[...] = jnp.concatenate(own, axis=1)
        next_ref[...] = jnp.concatenate(after, axis=1)


def filterbank(voltages, taps, channels):
    frame_len = taps.shape[1]
    steps = frame_len // CHUNK

    def frame(f):
        return pl.BlockSpec((HALF, CHUNK), lambda j, f=f: (0, f * steps + j))

    whole = pl.BlockSpec((ROWS, FRAMES * HALF), lambda j: (0, 0))
    out = jax.ShapeDtypeStruct((ROWS, FRAMES * HALF), jnp.float32)
    return pl.pallas_call(
        filterbank_kernel,
        grid=(steps,),
        in_specs=[pl.BlockSpec(memory_space=pltpu.SMEM)]
        + [frame(f) for f in range(FRAMES)]
        + [pl.BlockSpec((TAPS, CHUNK), lambda j: (0, j))],
        out_specs=[whole, whole],
        out_shape=[out, out],
        scratch_shapes=[
            pltpu.VMEM((ROWS, CHUNK), jnp.float32),
            pltpu.VMEM((ROWS, CHUNK), jnp.float32),
            pltpu.VMEM((ROWS, LANES), jnp.int32),
            pltpu.VMEM((2 * TAPS * ROWS, FRAMES * HALF), jnp.float32),
        ],
        compiler_params=pltpu.CompilerParams(vmem_limit_bytes=24 * 2**20),
        name="filterbank",
    )(channels, voltages, voltages, voltages, voltages, taps)


def combine_kernel(own_ref, before_ref, out_ref):
    total = own_ref[...] + before_ref[...]
    for c in range(4):
        rows = total[c * 8 : (c + 1) * 8]
        piece = jnp.concatenate([rows[:, :LANES], rows[:, LANES:]], axis=0).astype(jnp.bfloat16)
        for x in range(4):
            for y in range(4):
                out_ref[(x * 4 + c) * 4 + y] = piece


def combine(own, before):
    return pl.pallas_call(
        combine_kernel,
        out_shape=jax.ShapeDtypeStruct((64, 16, LANES), jnp.bfloat16),
        name="combine",
    )(own, before)


def arrange_kernel(got_ref, left_ref, right_ref):
    low = lax.broadcasted_iota(jnp.int32, (16, LANES), 1) < HALF

    def gathered(y):
        blocks = []
        for x in range(4):
            first, second = [], []
            for pair in range(2):
                even = got_ref[(x * 4 + 2 * pair) * 4 + y].astype(jnp.float32)
                odd = got_ref[(x * 4 + 2 * pair + 1) * 4 + y].astype(jnp.float32)
                first.append(jnp.where(low, even, pltpu.roll(odd, HALF, 1)))
                second.append(jnp.where(low, pltpu.roll(even, HALF, 1), odd))
            blocks += [jnp.concatenate(first, axis=1), jnp.concatenate(second, axis=1)]
        return jnp.concatenate(blocks, axis=0)

    right_ref[...] = gathered(lax.axis_index("x")).astype(jnp.bfloat16)
    left = gathered(lax.axis_index("y"))
    turned = []
    for g in range(16):
        rows = left[g * 8 : (g + 1) * 8]
        turned.append(pltpu.roll(rows, 4, 0))
    turned = jnp.concatenate(turned, axis=0)
    depth = lax.broadcasted_iota(jnp.int32, turned.shape, 0)
    turned = jnp.where(depth // 4 % 2 == 0, turned, -turned)
    lane = lax.broadcasted_iota(jnp.int32, (256, LANES), 1)
    for part, values in enumerate((left, turned)):
        flipped = values.T
        for c in range(4):
            left_ref[c, part] = jnp.where(lane % 4 == c, flipped, 0.0).astype(jnp.bfloat16)


def arrange(got):
    return pl.pallas_call(
        arrange_kernel,
        out_shape=[
            jax.ShapeDtypeStruct((4, 2, 256, LANES), jnp.bfloat16),
            jax.ShapeDtypeStruct((LANES, 256), jnp.bfloat16),
        ],
        name="arrange",
    )(got)


def correlate_kernel(scale, left_ref, right_ref, out_ref):
    right = right_ref[0]
    for c in range(4):
        for part in range(2):
            product = jnp.dot(left_ref[c, part], right, preferred_element_type=jnp.float32)
            out_ref[c, part] = (product * scale).astype(jnp.bfloat16)


def correlate(left, right, scale):
    return pl.pallas_call(
        functools.partial(correlate_kernel, scale),
        grid=(4,),
        in_specs=[
            pl.BlockSpec((4, 2, 256, LANES), lambda q: (0, 0, 0, 0)),
            pl.BlockSpec((1, LANES, 256), lambda q: (q, 0, 0)),
        ],
        out_specs=pl.BlockSpec((4, 2, 256, 256), lambda q: (0, 0, 0, q)),
        out_shape=jax.ShapeDtypeStruct((4, 2, 256, 1024), jnp.bfloat16),
        name="correlate",
    )(left, right)


def shards(voltages, taps, channels):
    own, after = filterbank(voltages, taps, channels)
    before = lax.ppermute(after, "x", [(i, i + 1) for i in range(3)])
    pieces = combine(own, before)
    got = lax.all_to_all(pieces, ("x", "zh", "y"), 0, 0, tiled=True)
    left, quarter = arrange(got)
    right = lax.all_gather(quarter, ("zl", "co"), axis=0)
    return correlate(left, right, 1.0 / 16.0)


def solution(mesh):
    fine = Mesh(mesh.devices.reshape(4, 4, 4, 2, 2), ("x", "zh", "y", "zl", "co"))
    placed = (P(("y", "zl", "co", "zh"), "x"), P(), P())
    return jax.shard_map(
        shards,
        mesh=fine,
        in_specs=placed,
        out_specs=P("zh", None, ("y", "zl", "co"), "x"),
        check_vma=False,
    )
```

```python
import functools
import math

import jax
import jax.numpy as jnp
from jax import lax
from jax.experimental import pallas as pl
from jax.experimental.pallas import tpu as pltpu
from jax.sharding import Mesh, PartitionSpec as P

FRAMES = 4
TAPS = 4
CHUNK = 4096
LANES = 128
ROWS = 32
HALF = 64
VMEM_LIMIT = 60 * 2**20
ARR_LIMIT = 16 * 2**20
CORR_LIMIT = 16 * 2**20


AXES = ("x", "zh", "y", "zl", "co")


def first_z():
    return 2 * lax.axis_index("zl") + lax.axis_index("co")


def first_x():
    return lax.axis_index("y")


def exchange_groups():
    groups = []
    for y in range(4):
        for zl in range(2):
            for co in range(2):
                members = [((p + y) % 4, (q + 2 * zl + co) % 4) for q in range(4) for p in range(4)]
                groups.append([(((x * 4 + z) * 4 + y) * 2 + zl) * 2 + co for x, z in members])
    return groups


def row_channels(chan_ref, shape):
    row = lax.broadcasted_iota(jnp.int32, shape, 0)
    which = row // 8 * 4 + row % 4
    chan = jnp.zeros(shape, jnp.int32)
    for c in range(16):
        chan = jnp.where(which == c, chan_ref[c], chan)
    return chan, row // 4 % 2


def filterbank_kernel(chan_ref, volt_ref, taps_ref, out_ref, frames_ref, coef_ref, cos_ref, sin_ref, base_ref, acc_ref, volt_sem, coef_sem):
    length = taps_ref.shape[1]
    steps = length // CHUNK
    turn = 2.0 * math.pi / length
    mask = length - 1

    def volt_copy(j, f):
        return pltpu.make_async_copy(
            volt_ref.at[:, pl.ds(pl.multiple_of(f * length + j * CHUNK, CHUNK), CHUNK)],
            frames_ref.at[j, pl.ds(f * HALF, HALF)],
            volt_sem.at[j, f],
        )

    def taps_copy(j):
        at = pl.ds(pl.multiple_of(j * CHUNK, CHUNK), CHUNK)
        return pltpu.make_async_copy(taps_ref.at[:, at], coef_ref.at[j], coef_sem.at[j])

    @pl.loop(0, steps)
    def _(j):
        for f in range(FRAMES):
            volt_copy(j, f).start()
        taps_copy(j).start()

    chan, part = row_channels(chan_ref, (ROWS, LANES))
    lane = lax.broadcasted_iota(jnp.int32, (ROWS, LANES), 1)

    def angles(index, shift):
        phase = ((index * chan + shift) & mask).astype(jnp.float32) * turn
        return jnp.cos(phase), jnp.sin(phase)

    fine_cos, fine_sin = angles(lane, 0)
    coarse_cos, coarse_sin = angles(lane * LANES, 0)
    for u in range(CHUNK // LANES):
        at = slice(u * LANES, (u + 1) * LANES)
        cu, su = coarse_cos[:, u : u + 1], coarse_sin[:, u : u + 1]
        cos_ref[:, at] = cu * fine_cos - su * fine_sin
        sin_ref[:, at] = su * fine_cos + cu * fine_sin
    base_cos, base_sin = angles(lane * CHUNK, part * (length // 4))
    scale = 1.0 / math.sqrt(length)
    base_cos, base_sin = base_cos * scale, base_sin * scale

    for j in range(steps):
        base_ref[j] = jnp.broadcast_to(base_cos[:, j : j + 1], (ROWS, LANES))
        base_ref[steps + j] = jnp.broadcast_to(base_sin[:, j : j + 1], (ROWS, LANES))
    acc_ref[...] = jnp.zeros_like(acc_ref)

    def chunk(j, carry):
        taps_copy(j).wait()
        for f in range(FRAMES):
            volt_copy(j, f).wait()
        turn_cos, turn_sin = base_ref[j], base_ref[steps + j]
        high, low = [], []
        for u in range(CHUNK // LANES):
            at = slice(u * LANES, (u + 1) * LANES)
            table = turn_cos * cos_ref[:, at] - turn_sin * sin_ref[:, at]
            w = jnp.concatenate([table * coef_ref[j, t : t + 1, at] for t in range(TAPS)], axis=0)
            h = w.astype(jnp.bfloat16)
            high.append(h)
            low.append((w - h.astype(jnp.float32)).astype(jnp.bfloat16))
        weights = jnp.concatenate(
            [jnp.concatenate(high, axis=1), jnp.concatenate(low, axis=1)], axis=0
        )
        acc_ref[...] = acc_ref[...] + lax.dot_general(
            weights, frames_ref[j], (((1,), (1,)), ((), ())), preferred_element_type=jnp.float32
        )
        return carry

    lax.fori_loop(0, steps, chunk, 0)
    g = acc_ref[: TAPS * ROWS] + acc_ref[TAPS * ROWS :]

    def term(t, f):
        return g[t * ROWS : (t + 1) * ROWS, f * HALF : (f + 1) * HALF]

    own, after = [], []
    for s in range(FRAMES):
        own.append(sum(term(f - s + 3, f) for f in range(s + 1)))
        if s < TAPS - 1:
            after.append(sum(term(f - 1 - s, f) for f in range(s + 1, FRAMES)))
    after.append(jnp.zeros_like(after[0]))
    own = jnp.concatenate(own, axis=1)
    after = jnp.concatenate(after, axis=1)
    for c in range(4):
        rows = slice(c * 8, (c + 1) * 8)
        piece = [part[rows, at : at + LANES] for part in (own, after) for at in (0, LANES)]
        piece = jnp.concatenate(piece, axis=0)
        place = (c - first_z()) % 4
        for x in range(4):
            out_ref[place * 4 + x] = piece


def filterbank(voltages, taps, channels):
    steps = taps.shape[1] // CHUNK
    return pl.pallas_call(
        filterbank_kernel,
        in_specs=[
            pl.BlockSpec(memory_space=pltpu.SMEM),
            pl.BlockSpec(memory_space=pl.ANY),
            pl.BlockSpec(memory_space=pl.ANY),
        ],
        out_shape=jax.ShapeDtypeStruct((16, 32, LANES), jnp.float32),
        scratch_shapes=[
            pltpu.VMEM((steps, FRAMES * HALF, CHUNK), jnp.bfloat16),
            pltpu.VMEM((steps, TAPS, CHUNK), jnp.float32),
            pltpu.VMEM((ROWS, CHUNK), jnp.float32),
            pltpu.VMEM((ROWS, CHUNK), jnp.float32),
            pltpu.VMEM((2 * steps, ROWS, LANES), jnp.float32),
            pltpu.VMEM((2 * TAPS * ROWS, FRAMES * HALF), jnp.float32),
            pltpu.SemaphoreType.DMA((steps, FRAMES)),
            pltpu.SemaphoreType.DMA((steps,)),
        ],
        compiler_params=pltpu.CompilerParams(vmem_limit_bytes=VMEM_LIMIT),
        name="filterbank",
    )(channels, voltages, taps)


def arrange_kernel(got_ref, rows_ref):
    low = lax.broadcasted_iota(jnp.int32, (8, LANES), 1) < HALF

    turn_x, turn_z = first_x(), first_z()

    def spectra(x, col, late):
        def part(x, at):
            place = (col - turn_z) % 4 * 4 + (x - turn_x) % 4
            return got_ref[place, pl.ds(at, 8)]

        total = part(x, 8 * late)
        if x > 0:
            total = total + part(x - 1, 16 + 8 * late)
        return total.astype(jnp.bfloat16).astype(jnp.float32)

    for x in range(4):
        first, second = [], []
        for late in range(2):
            a, b = [], []
            for pair in range(2):
                even = spectra(x, 2 * pair, late)
                odd = spectra(x, 2 * pair + 1, late)
                a.append(jnp.where(low, even, pltpu.roll(odd, HALF, 1)))
                b.append(jnp.where(low, pltpu.roll(even, HALF, 1), odd))
            first.append(jnp.concatenate(a, axis=1))
            second.append(jnp.concatenate(b, axis=1))
        block = jnp.concatenate(first + second, axis=0)
        rows_ref[32 * x : 32 * (x + 1)] = block.astype(jnp.bfloat16)


def arrange(got):
    return pl.pallas_call(
        arrange_kernel,
        out_shape=jax.ShapeDtypeStruct((LANES, 256), jnp.bfloat16),
        compiler_params=pltpu.CompilerParams(vmem_limit_bytes=ARR_LIMIT),
        name="arrange",
    )(got)


def correlate_kernel(scale, rows_ref, near_ref, near_other_ref, far_ref, far_other_ref, out_ref, left_ref, right_ref, held_ref, sem):
    left = rows_ref[...].astype(jnp.float32)
    turned = [pltpu.roll(left[g * 8 : (g + 1) * 8], 4, 0) for g in range(LANES // 8)]
    turned = jnp.concatenate(turned, axis=0)
    depth = lax.broadcasted_iota(jnp.int32, turned.shape, 0)
    turned = jnp.where(depth // 4 % 2 == 0, turned, -turned)
    left_ref[0] = left.T
    left_ref[1] = turned.T
    width = near_ref.shape[1]
    mine = 2 * lax.axis_index("zl") + lax.axis_index("co")
    for k, block in enumerate((near_ref, near_other_ref, far_ref, far_other_ref)):
        for place in range(4):
            @pl.when(mine == place ^ k)
            def _():
                right_ref[:, place * width : (place + 1) * width] = block[...]

    lane = lax.broadcasted_iota(jnp.int32, left_ref.shape[1:], 1)

    def copy(k):
        return pltpu.make_async_copy(held_ref.at[k], out_ref.at[k // 2, k % 2], sem.at[k])

    @pl.loop(0, 8)
    def _(k):
        chosen = jnp.where(lane % 4 == k // 2, left_ref[k % 2], 0.0).astype(jnp.bfloat16)
        product = jnp.dot(chosen, right_ref[...], preferred_element_type=jnp.float32)
        held_ref[k] = (product * scale).astype(jnp.bfloat16)
        copy(k).start()

    @pl.loop(0, 8)
    def _(k):
        copy(k).wait()


def correlate(rows, blocks, scale):
    depth, width = rows.shape
    return pl.pallas_call(
        functools.partial(correlate_kernel, scale),
        in_specs=[pl.BlockSpec(memory_space=pltpu.VMEM)] * 5,
        out_specs=pl.BlockSpec(memory_space=pl.ANY),
        out_shape=jax.ShapeDtypeStruct((4, 2, width, 4 * width), jnp.bfloat16),
        scratch_shapes=[
            pltpu.VMEM((2, width, depth), jnp.float32),
            pltpu.VMEM((depth, 4 * width), jnp.bfloat16),
            pltpu.VMEM((8, width, 4 * width), jnp.bfloat16),
            pltpu.SemaphoreType.DMA((8,)),
        ],
        compiler_params=pltpu.CompilerParams(vmem_limit_bytes=CORR_LIMIT),
        name="correlate",
    )(rows, *blocks)


def across():
    pairs = []
    for x in range(4):
        for y in range(4):
            source = (x + 2 - (y - x)) % 4
            pairs.append((source * 4 + x, x * 4 + y))
    return pairs


def shards(voltages, taps, channels):
    pieces = filterbank(voltages, taps, channels)
    got = lax.all_to_all(pieces, AXES, 0, 0, axis_index_groups=exchange_groups(), tiled=True)
    rows = arrange(got)
    swap = [(0, 1), (1, 0)]
    pairs = [(2 * s + z, 2 * d + 1 - z) for s, d in across() for z in range(2)]
    near = lax.ppermute(rows, ("x", "y"), across())
    far = lax.ppermute(rows, ("x", "y", "zl"), pairs)
    near_other = lax.ppermute(near, "co", swap)
    far_other = lax.ppermute(far, "co", swap)
    return correlate(rows, (near, near_other, far, far_other), 1.0 / 16.0)


def solution(mesh):
    fine = Mesh(mesh.devices.reshape(4, 4, 4, 2, 2), ("x", "zh", "y", "zl", "co"))
    placed = (P(("y", "zl", "co", "zh"), "x"), P(), P())
    return jax.shard_map(
        shards,
        mesh=fine,
        in_specs=placed,
        out_specs=P("zh", None, ("y", "zl", "co"), "x"),
        check_vma=False,
    )
```

```python
import functools
import math

import jax
import jax.numpy as jnp
from jax import lax
from jax.experimental import pallas as pl
from jax.experimental.pallas import tpu as pltpu
from jax.sharding import Mesh, PartitionSpec as P

FRAMES = 4
TAPS = 4
CHUNK = 4096
LANES = 128
ROWS = 32
HALF = 64
VMEM_LIMIT = 60 * 2**20
SMALL_LIMIT = 16 * 2**20


AXES = ("x", "zh", "y", "zl", "co")
FIRST = 2


def exchange_groups():
    groups = []
    for y in range(4):
        for zl in range(2):
            for co in range(2):
                members = [((p + FIRST) % 4, (q + FIRST) % 4) for q in range(4) for p in range(4)]
                groups.append([(((x * 4 + z) * 4 + y) * 2 + zl) * 2 + co for x, z in members])
    return groups


def row_channels(chan_ref, shape):
    row = lax.broadcasted_iota(jnp.int32, shape, 0)
    which = row // 8 * 4 + row % 4
    chan = jnp.zeros(shape, jnp.int32)
    for c in range(16):
        chan = jnp.where(which == c, chan_ref[c], chan)
    return chan, row // 4 % 2


def filterbank_kernel(chan_ref, volt_ref, taps_ref, out_ref, frames_ref, coef_ref, cos_ref, sin_ref, base_ref, acc_ref, volt_sem, coef_sem):
    length = taps_ref.shape[1]
    steps = length // CHUNK
    turn = 2.0 * math.pi / length
    mask = length - 1

    def volt_copy(j, f):
        return pltpu.make_async_copy(
            volt_ref.at[:, pl.ds(pl.multiple_of(f * length + j * CHUNK, CHUNK), CHUNK)],
            frames_ref.at[j, pl.ds(f * HALF, HALF)],
            volt_sem.at[j, f],
        )

    def taps_copy(j):
        at = pl.ds(pl.multiple_of(j * CHUNK, CHUNK), CHUNK)
        return pltpu.make_async_copy(taps_ref.at[:, at], coef_ref.at[j], coef_sem.at[j])

    @pl.loop(0, steps)
    def _(j):
        for f in range(FRAMES):
            volt_copy(j, f).start()
        taps_copy(j).start()

    chan, part = row_channels(chan_ref, (ROWS, LANES))
    lane = lax.broadcasted_iota(jnp.int32, (ROWS, LANES), 1)

    def angles(index, shift):
        phase = ((index * chan + shift) & mask).astype(jnp.float32) * turn
        return jnp.cos(phase), jnp.sin(phase)

    fine_cos, fine_sin = angles(lane, 0)
    coarse_cos, coarse_sin = angles(lane * LANES, 0)
    for u in range(CHUNK // LANES):
        at = slice(u * LANES, (u + 1) * LANES)
        cu, su = coarse_cos[:, u : u + 1], coarse_sin[:, u : u + 1]
        cos_ref[:, at] = cu * fine_cos - su * fine_sin
        sin_ref[:, at] = su * fine_cos + cu * fine_sin
    base_cos, base_sin = angles(lane * CHUNK, part * (length // 4))
    scale = 1.0 / math.sqrt(length)
    base_cos, base_sin = base_cos * scale, base_sin * scale

    for j in range(steps):
        base_ref[j] = jnp.broadcast_to(base_cos[:, j : j + 1], (ROWS, LANES))
        base_ref[steps + j] = jnp.broadcast_to(base_sin[:, j : j + 1], (ROWS, LANES))
    acc_ref[...] = jnp.zeros_like(acc_ref)

    def chunk(j, carry):
        taps_copy(j).wait()
        for f in range(FRAMES):
            volt_copy(j, f).wait()
        turn_cos, turn_sin = base_ref[j], base_ref[steps + j]
        high, low = [], []
        for u in range(CHUNK // LANES):
            at = slice(u * LANES, (u + 1) * LANES)
            table = turn_cos * cos_ref[:, at] - turn_sin * sin_ref[:, at]
            w = jnp.concatenate([table * coef_ref[j, t : t + 1, at] for t in range(TAPS)], axis=0)
            h = w.astype(jnp.bfloat16)
            high.append(h)
            low.append((w - h.astype(jnp.float32)).astype(jnp.bfloat16))
        weights = jnp.concatenate(
            [jnp.concatenate(high, axis=1), jnp.concatenate(low, axis=1)], axis=0
        )
        acc_ref[...] = acc_ref[...] + lax.dot_general(
            weights, frames_ref[j], (((1,), (1,)), ((), ())), preferred_element_type=jnp.float32
        )
        return carry

    lax.fori_loop(0, steps, chunk, 0)
    g = acc_ref[: TAPS * ROWS] + acc_ref[TAPS * ROWS :]

    def term(t, f):
        return g[t * ROWS : (t + 1) * ROWS, f * HALF : (f + 1) * HALF]

    own, after = [], []
    for s in range(FRAMES):
        own.append(sum(term(f - s + 3, f) for f in range(s + 1)))
        if s < TAPS - 1:
            after.append(sum(term(f - 1 - s, f) for f in range(s + 1, FRAMES)))
    after.append(jnp.zeros_like(after[0]))
    own = jnp.concatenate(own, axis=1)
    after = jnp.concatenate(after, axis=1)
    for c in range(4):
        rows = slice(c * 8, (c + 1) * 8)
        piece = [part[rows, at : at + LANES] for part in (own, after) for at in (0, LANES)]
        piece = jnp.concatenate(piece, axis=0)
        place = (c - FIRST) % 4
        for x in range(4):
            out_ref[place * 4 + x] = piece


def filterbank(voltages, taps, channels):
    steps = taps.shape[1] // CHUNK
    return pl.pallas_call(
        filterbank_kernel,
        in_specs=[
            pl.BlockSpec(memory_space=pltpu.SMEM),
            pl.BlockSpec(memory_space=pl.ANY),
            pl.BlockSpec(memory_space=pl.ANY),
        ],
        out_shape=jax.ShapeDtypeStruct((16, 32, LANES), jnp.float32),
        scratch_shapes=[
            pltpu.VMEM((steps, FRAMES * HALF, CHUNK), jnp.bfloat16),
            pltpu.VMEM((steps, TAPS, CHUNK), jnp.float32),
            pltpu.VMEM((ROWS, CHUNK), jnp.float32),
            pltpu.VMEM((ROWS, CHUNK), jnp.float32),
            pltpu.VMEM((2 * steps, ROWS, LANES), jnp.float32),
            pltpu.VMEM((2 * TAPS * ROWS, FRAMES * HALF), jnp.float32),
            pltpu.SemaphoreType.DMA((steps, FRAMES)),
            pltpu.SemaphoreType.DMA((steps,)),
        ],
        compiler_params=pltpu.CompilerParams(vmem_limit_bytes=VMEM_LIMIT),
        name="filterbank",
    )(channels, voltages, taps)


def arrange_kernel(got_ref, rows_ref):
    low = lax.broadcasted_iota(jnp.int32, (8, LANES), 1) < HALF

    def spectra(x, col, late):
        def part(x, at):
            place = (col - FIRST) % 4 * 4 + (x - FIRST) % 4
            return got_ref[place, pl.ds(at, 8)]

        total = part(x, 8 * late)
        if x > 0:
            total = total + part(x - 1, 16 + 8 * late)
        return total.astype(jnp.bfloat16).astype(jnp.float32)

    for x in range(4):
        first, second = [], []
        for late in range(2):
            a, b = [], []
            for pair in range(2):
                even = spectra(x, 2 * pair, late)
                odd = spectra(x, 2 * pair + 1, late)
                a.append(jnp.where(low, even, pltpu.roll(odd, HALF, 1)))
                b.append(jnp.where(low, pltpu.roll(even, HALF, 1), odd))
            first.append(jnp.concatenate(a, axis=1))
            second.append(jnp.concatenate(b, axis=1))
        block = jnp.concatenate(first + second, axis=0)
        rows_ref[32 * x : 32 * (x + 1)] = block.astype(jnp.bfloat16)


def arrange(got):
    return pl.pallas_call(
        arrange_kernel,
        out_shape=jax.ShapeDtypeStruct((LANES, 256), jnp.bfloat16),
        compiler_params=pltpu.CompilerParams(vmem_limit_bytes=SMALL_LIMIT),
        name="arrange",
    )(got)


def correlate_kernel(scale, rows_ref, near_ref, near_other_ref, far_ref, far_other_ref, out_ref, left_ref, right_ref, held_ref, sem):
    left = rows_ref[...].astype(jnp.float32)
    turned = [pltpu.roll(left[g * 8 : (g + 1) * 8], 4, 0) for g in range(LANES // 8)]
    turned = jnp.concatenate(turned, axis=0)
    depth = lax.broadcasted_iota(jnp.int32, turned.shape, 0)
    turned = jnp.where(depth // 4 % 2 == 0, turned, -turned)
    left_ref[0] = left.T
    left_ref[1] = turned.T
    width = near_ref.shape[1]
    mine = 2 * lax.axis_index("zl") + lax.axis_index("co")
    for k, block in enumerate((near_ref, near_other_ref, far_ref, far_other_ref)):
        for place in range(4):
            @pl.when(mine == place ^ k)
            def _():
                right_ref[:, place * width : (place + 1) * width] = block[...]

    lane = lax.broadcasted_iota(jnp.int32, left_ref.shape[1:], 1)

    def copy(k):
        return pltpu.make_async_copy(held_ref.at[k], out_ref.at[k // 2, k % 2], sem.at[k])

    for k in range(8):
        chosen = jnp.where(lane % 4 == k // 2, left_ref[k % 2], 0.0).astype(jnp.bfloat16)
        product = jnp.dot(chosen, right_ref[...], preferred_element_type=jnp.float32)
        held_ref[k] = (product * scale).astype(jnp.bfloat16)
        copy(k).start()
    for k in range(8):
        copy(k).wait()


def correlate(rows, blocks, scale):
    depth, width = rows.shape
    return pl.pallas_call(
        functools.partial(correlate_kernel, scale),
        in_specs=[pl.BlockSpec(memory_space=pltpu.VMEM)] * 5,
        out_specs=pl.BlockSpec(memory_space=pl.ANY),
        out_shape=jax.ShapeDtypeStruct((4, 2, width, 4 * width), jnp.bfloat16),
        scratch_shapes=[
            pltpu.VMEM((2, width, depth), jnp.float32),
            pltpu.VMEM((depth, 4 * width), jnp.bfloat16),
            pltpu.VMEM((8, width, 4 * width), jnp.bfloat16),
            pltpu.SemaphoreType.DMA((8,)),
        ],
        compiler_params=pltpu.CompilerParams(vmem_limit_bytes=SMALL_LIMIT),
        name="correlate",
    )(rows, *blocks)


def across_near():
    pairs = []
    for x in range(4):
        for y in range(4):
            source = (x + 2 - (y - x)) % 4
            pairs.append((source * 4 + x, x * 4 + y))
    return pairs


def across_far():
    pairs = []
    for x in range(4):
        for y in range(4):
            source = (x + 2 + (y - x)) % 4
            pairs.append((source * 4 + x, x * 4 + y))
    return pairs


def shards(voltages, taps, channels):
    pieces = filterbank(voltages, taps, channels)
    got = lax.all_to_all(pieces, AXES, 0, 0, axis_index_groups=exchange_groups(), tiled=True)
    rows = arrange(got)
    swap = [(0, 1), (1, 0)]
    pairs = [(2 * s + z, 2 * d + 1 - z) for s, d in across_far() for z in range(2)]
    near = lax.ppermute(rows, ("x", "y"), across_near())
    far = lax.ppermute(rows, ("x", "y", "zl"), pairs)
    near_other = lax.ppermute(near, "co", swap)
    far_other = lax.ppermute(far, "co", swap)
    return correlate(rows, (near, near_other, far, far_other), 1.0 / 16.0)


def solution(mesh):
    fine = Mesh(mesh.devices.reshape(4, 4, 4, 2, 2), ("x", "zh", "y", "zl", "co"))
    placed = (P(("y", "zl", "co", "zh"), "x"), P(), P())
    return jax.shard_map(
        shards,
        mesh=fine,
        in_specs=placed,
        out_specs=P("zh", None, ("y", "zl", "co"), "x"),
        check_vma=False,
    )
```

```python
import functools
import math

import jax
import jax.numpy as jnp
from jax import lax
from jax.experimental import pallas as pl
from jax.experimental.pallas import tpu as pltpu
from jax.sharding import Mesh, PartitionSpec as P

FRAMES = 4
TAPS = 4
CHUNK = 4096
LANES = 128
ROWS = 32
HALF = 64
VMEM_LIMIT = 60 * 2**20
SMALL_LIMIT = 16 * 2**20


AXES = ("x", "zh", "y", "zl", "co")
Z_ORDER = (2, 0, 3, 1)
X_ORDER = (2, 3, 0, 1)


def exchange_groups():
    groups = []
    for y in range(4):
        for zl in range(2):
            for co in range(2):
                members = [(x, z) for z in Z_ORDER for x in X_ORDER]
                groups.append([(((x * 4 + z) * 4 + y) * 2 + zl) * 2 + co for x, z in members])
    return groups


def row_channels(chan_ref, shape):
    row = lax.broadcasted_iota(jnp.int32, shape, 0)
    which = row // 8 * 4 + row % 4
    chan = jnp.zeros(shape, jnp.int32)
    for c in range(16):
        chan = jnp.where(which == c, chan_ref[c], chan)
    return chan, row // 4 % 2


def filterbank_kernel(chan_ref, volt_ref, taps_ref, out_ref, frames_ref, coef_ref, cos_ref, sin_ref, base_ref, acc_ref, volt_sem, coef_sem):
    length = taps_ref.shape[1]
    steps = length // CHUNK
    turn = 2.0 * math.pi / length
    mask = length - 1

    def volt_copy(j, f):
        return pltpu.make_async_copy(
            volt_ref.at[:, pl.ds(pl.multiple_of(f * length + j * CHUNK, CHUNK), CHUNK)],
            frames_ref.at[j, pl.ds(f * HALF, HALF)],
            volt_sem.at[j, f],
        )

    def taps_copy(j):
        at = pl.ds(pl.multiple_of(j * CHUNK, CHUNK), CHUNK)
        return pltpu.make_async_copy(taps_ref.at[:, at], coef_ref.at[j], coef_sem.at[j])

    @pl.loop(0, steps)
    def _(j):
        for f in range(FRAMES):
            volt_copy(j, f).start()
        taps_copy(j).start()

    chan, part = row_channels(chan_ref, (ROWS, LANES))
    lane = lax.broadcasted_iota(jnp.int32, (ROWS, LANES), 1)

    def angles(index, shift):
        phase = ((index * chan + shift) & mask).astype(jnp.float32) * turn
        return jnp.cos(phase), jnp.sin(phase)

    fine_cos, fine_sin = angles(lane, 0)
    coarse_cos, coarse_sin = angles(lane * LANES, 0)
    for u in range(CHUNK // LANES):
        at = slice(u * LANES, (u + 1) * LANES)
        cu, su = coarse_cos[:, u : u + 1], coarse_sin[:, u : u + 1]
        cos_ref[:, at] = cu * fine_cos - su * fine_sin
        sin_ref[:, at] = su * fine_cos + cu * fine_sin
    base_cos, base_sin = angles(lane * CHUNK, part * (length // 4))
    scale = 1.0 / math.sqrt(length)
    base_cos, base_sin = base_cos * scale, base_sin * scale

    for j in range(steps):
        base_ref[j] = jnp.broadcast_to(base_cos[:, j : j + 1], (ROWS, LANES))
        base_ref[steps + j] = jnp.broadcast_to(base_sin[:, j : j + 1], (ROWS, LANES))
    acc_ref[...] = jnp.zeros_like(acc_ref)

    def chunk(j, carry):
        taps_copy(j).wait()
        for f in range(FRAMES):
            volt_copy(j, f).wait()
        turn_cos, turn_sin = base_ref[j], base_ref[steps + j]
        high, low = [], []
        for u in range(CHUNK // LANES):
            at = slice(u * LANES, (u + 1) * LANES)
            table = turn_cos * cos_ref[:, at] - turn_sin * sin_ref[:, at]
            w = jnp.concatenate([table * coef_ref[j, t : t + 1, at] for t in range(TAPS)], axis=0)
            h = w.astype(jnp.bfloat16)
            high.append(h)
            low.append((w - h.astype(jnp.float32)).astype(jnp.bfloat16))
        weights = jnp.concatenate(
            [jnp.concatenate(high, axis=1), jnp.concatenate(low, axis=1)], axis=0
        )
        acc_ref[...] = acc_ref[...] + lax.dot_general(
            weights, frames_ref[j], (((1,), (1,)), ((), ())), preferred_element_type=jnp.float32
        )
        return carry

    lax.fori_loop(0, steps, chunk, 0)
    g = acc_ref[: TAPS * ROWS] + acc_ref[TAPS * ROWS :]

    def term(t, f):
        return g[t * ROWS : (t + 1) * ROWS, f * HALF : (f + 1) * HALF]

    own, after = [], []
    for s in range(FRAMES):
        own.append(sum(term(f - s + 3, f) for f in range(s + 1)))
        if s < TAPS - 1:
            after.append(sum(term(f - 1 - s, f) for f in range(s + 1, FRAMES)))
    after.append(jnp.zeros_like(after[0]))
    own = jnp.concatenate(own, axis=1)
    after = jnp.concatenate(after, axis=1)
    for c in range(4):
        rows = slice(c * 8, (c + 1) * 8)
        piece = [part[rows, at : at + LANES] for part in (own, after) for at in (0, LANES)]
        piece = jnp.concatenate(piece, axis=0)
        place = Z_ORDER.index(c)
        for x in range(4):
            out_ref[place * 4 + x] = piece


def filterbank(voltages, taps, channels):
    steps = taps.shape[1] // CHUNK
    return pl.pallas_call(
        filterbank_kernel,
        in_specs=[
            pl.BlockSpec(memory_space=pltpu.SMEM),
            pl.BlockSpec(memory_space=pl.ANY),
            pl.BlockSpec(memory_space=pl.ANY),
        ],
        out_shape=jax.ShapeDtypeStruct((16, 32, LANES), jnp.float32),
        scratch_shapes=[
            pltpu.VMEM((steps, FRAMES * HALF, CHUNK), jnp.bfloat16),
            pltpu.VMEM((steps, TAPS, CHUNK), jnp.float32),
            pltpu.VMEM((ROWS, CHUNK), jnp.float32),
            pltpu.VMEM((ROWS, CHUNK), jnp.float32),
            pltpu.VMEM((2 * steps, ROWS, LANES), jnp.float32),
            pltpu.VMEM((2 * TAPS * ROWS, FRAMES * HALF), jnp.float32),
            pltpu.SemaphoreType.DMA((steps, FRAMES)),
            pltpu.SemaphoreType.DMA((steps,)),
        ],
        compiler_params=pltpu.CompilerParams(vmem_limit_bytes=VMEM_LIMIT),
        name="filterbank",
    )(channels, voltages, taps)


def arrange_kernel(got_ref, rows_ref):
    low = lax.broadcasted_iota(jnp.int32, (8, LANES), 1) < HALF

    def spectra(x, col, late):
        def part(x, at):
            place = Z_ORDER.index(col) * 4 + X_ORDER.index(x)
            return got_ref[place, pl.ds(at, 8)]

        total = part(x, 8 * late)
        if x > 0:
            total = total + part(x - 1, 16 + 8 * late)
        return total.astype(jnp.bfloat16).astype(jnp.float32)

    for x in range(4):
        first, second = [], []
        for late in range(2):
            a, b = [], []
            for pair in range(2):
                even = spectra(x, 2 * pair, late)
                odd = spectra(x, 2 * pair + 1, late)
                a.append(jnp.where(low, even, pltpu.roll(odd, HALF, 1)))
                b.append(jnp.where(low, pltpu.roll(even, HALF, 1), odd))
            first.append(jnp.concatenate(a, axis=1))
            second.append(jnp.concatenate(b, axis=1))
        block = jnp.concatenate(first + second, axis=0)
        rows_ref[32 * x : 32 * (x + 1)] = block.astype(jnp.bfloat16)


def arrange(got):
    return pl.pallas_call(
        arrange_kernel,
        out_shape=jax.ShapeDtypeStruct((LANES, 256), jnp.bfloat16),
        compiler_params=pltpu.CompilerParams(vmem_limit_bytes=SMALL_LIMIT),
        name="arrange",
    )(got)


def correlate_kernel(scale, rows_ref, near_ref, near_other_ref, far_ref, far_other_ref, out_ref, left_ref, right_ref, held_ref, sem):
    left = rows_ref[...].astype(jnp.float32)
    turned = [pltpu.roll(left[g * 8 : (g + 1) * 8], 4, 0) for g in range(LANES // 8)]
    turned = jnp.concatenate(turned, axis=0)
    depth = lax.broadcasted_iota(jnp.int32, turned.shape, 0)
    turned = jnp.where(depth // 4 % 2 == 0, turned, -turned)
    left_ref[0] = left.T
    left_ref[1] = turned.T
    width = near_ref.shape[1]
    mine = 2 * lax.axis_index("zl") + lax.axis_index("co")
    for k, block in enumerate((near_ref, near_other_ref, far_ref, far_other_ref)):
        for place in range(4):
            @pl.when(mine == place ^ k)
            def _():
                right_ref[:, place * width : (place + 1) * width] = block[...]

    lane = lax.broadcasted_iota(jnp.int32, left_ref.shape[1:], 1)

    def copy(k):
        return pltpu.make_async_copy(held_ref.at[k], out_ref.at[k // 2, k % 2], sem.at[k])

    for k in range(8):
        chosen = jnp.where(lane % 4 == k // 2, left_ref[k % 2], 0.0).astype(jnp.bfloat16)
        product = jnp.dot(chosen, right_ref[...], preferred_element_type=jnp.float32)
        held_ref[k] = (product * scale).astype(jnp.bfloat16)
        copy(k).start()
    for k in range(8):
        copy(k).wait()


def correlate(rows, blocks, scale):
    depth, width = rows.shape
    return pl.pallas_call(
        functools.partial(correlate_kernel, scale),
        in_specs=[pl.BlockSpec(memory_space=pltpu.VMEM)] * 5,
        out_specs=pl.BlockSpec(memory_space=pl.ANY),
        out_shape=jax.ShapeDtypeStruct((4, 2, width, 4 * width), jnp.bfloat16),
        scratch_shapes=[
            pltpu.VMEM((2, width, depth), jnp.float32),
            pltpu.VMEM((depth, 4 * width), jnp.bfloat16),
            pltpu.VMEM((8, width, 4 * width), jnp.bfloat16),
            pltpu.SemaphoreType.DMA((8,)),
        ],
        compiler_params=pltpu.CompilerParams(vmem_limit_bytes=SMALL_LIMIT),
        name="correlate",
    )(rows, *blocks)


def across_near():
    pairs = []
    for x in range(4):
        for y in range(4):
            source = (x + 2 - (y - x)) % 4
            pairs.append((source * 4 + x, x * 4 + y))
    return pairs


def across_far():
    pairs = []
    for x in range(4):
        for y in range(4):
            source = (x + 2 + (y - x)) % 4
            pairs.append((source * 4 + x, x * 4 + y))
    return pairs


def shards(voltages, taps, channels):
    pieces = filterbank(voltages, taps, channels)
    got = lax.all_to_all(pieces, AXES, 0, 0, axis_index_groups=exchange_groups(), tiled=True)
    rows = arrange(got)
    swap = [(0, 1), (1, 0)]
    pairs = [(2 * s + z, 2 * d + 1 - z) for s, d in across_far() for z in range(2)]
    near = lax.ppermute(rows, ("x", "y"), across_near())
    far = lax.ppermute(rows, ("x", "y", "zl"), pairs)
    near_other = lax.ppermute(near, "co", swap)
    far_other = lax.ppermute(far, "co", swap)
    return correlate(rows, (near, near_other, far, far_other), 1.0 / 16.0)


def solution(mesh):
    fine = Mesh(mesh.devices.reshape(4, 4, 4, 2, 2), ("x", "zh", "y", "zl", "co"))
    placed = (P(("y", "zl", "co", "zh"), "x"), P(), P())
    return jax.shard_map(
        shards,
        mesh=fine,
        in_specs=placed,
        out_specs=P("zh", None, ("y", "zl", "co"), "x"),
        check_vma=False,
    )
```

```python
import functools
import math

import jax
import jax.numpy as jnp
from jax import lax
from jax.experimental import pallas as pl
from jax.experimental.pallas import tpu as pltpu
from jax.sharding import Mesh, PartitionSpec as P

FRAMES = 4
TAPS = 4
CHUNK = 4096
LANES = 128
ROWS = 32
HALF = 64
VMEM_LIMIT = 60 * 2**20
SMALL_LIMIT = 16 * 2**20


AXES = ("x", "zh", "y", "zl", "co")
Z_ORDER = (2, 0, 3, 1)
X_ORDER = (2, 3, 0, 1)


def exchange_groups():
    groups = []
    for y in range(4):
        for zl in range(2):
            for co in range(2):
                members = [(x, z) for z in Z_ORDER for x in X_ORDER]
                groups.append([(((x * 4 + z) * 4 + y) * 2 + zl) * 2 + co for x, z in members])
    return groups


def row_channels(chan_ref, shape):
    row = lax.broadcasted_iota(jnp.int32, shape, 0)
    which = row // 8 * 4 + row % 4
    chan = jnp.zeros(shape, jnp.int32)
    for c in range(16):
        chan = jnp.where(which == c, chan_ref[c], chan)
    return chan, row // 4 % 2


def filterbank_kernel(chan_ref, volt_ref, taps_ref, out_ref, frames_ref, coef_ref, cos_ref, sin_ref, base_ref, acc_ref, volt_sem, coef_sem):
    length = taps_ref.shape[1]
    steps = length // CHUNK
    turn = 2.0 * math.pi / length
    mask = length - 1

    def volt_copy(j, f):
        return pltpu.make_async_copy(
            volt_ref.at[:, pl.ds(pl.multiple_of(f * length + j * CHUNK, CHUNK), CHUNK)],
            frames_ref.at[j, pl.ds(f * HALF, HALF)],
            volt_sem.at[j, f],
        )

    def taps_copy(j):
        at = pl.ds(pl.multiple_of(j * CHUNK, CHUNK), CHUNK)
        return pltpu.make_async_copy(taps_ref.at[:, at], coef_ref.at[j], coef_sem.at[j])

    @pl.loop(0, steps)
    def _(j):
        for f in range(FRAMES):
            volt_copy(j, f).start()
        taps_copy(j).start()

    chan, part = row_channels(chan_ref, (ROWS, LANES))
    lane = lax.broadcasted_iota(jnp.int32, (ROWS, LANES), 1)

    def angles(index, shift):
        phase = ((index * chan + shift) & mask).astype(jnp.float32) * turn
        return jnp.cos(phase), jnp.sin(phase)

    fine_cos, fine_sin = angles(lane, 0)
    coarse_cos, coarse_sin = angles(lane * LANES, 0)
    for u in range(CHUNK // LANES):
        at = slice(u * LANES, (u + 1) * LANES)
        cu, su = coarse_cos[:, u : u + 1], coarse_sin[:, u : u + 1]
        cos_ref[:, at] = cu * fine_cos - su * fine_sin
        sin_ref[:, at] = su * fine_cos + cu * fine_sin
    base_cos, base_sin = angles(lane * CHUNK, part * (length // 4))
    scale = 1.0 / math.sqrt(length)
    base_cos, base_sin = base_cos * scale, base_sin * scale

    for j in range(steps):
        base_ref[j] = jnp.broadcast_to(base_cos[:, j : j + 1], (ROWS, LANES))
        base_ref[steps + j] = jnp.broadcast_to(base_sin[:, j : j + 1], (ROWS, LANES))
    acc_ref[...] = jnp.zeros_like(acc_ref)

    def chunk(j, carry):
        taps_copy(j).wait()
        for f in range(FRAMES):
            volt_copy(j, f).wait()
        turn_cos, turn_sin = base_ref[j], base_ref[steps + j]
        high, low = [], []
        for u in range(CHUNK // LANES):
            at = slice(u * LANES, (u + 1) * LANES)
            table = turn_cos * cos_ref[:, at] - turn_sin * sin_ref[:, at]
            w = jnp.concatenate([table * coef_ref[j, t : t + 1, at] for t in range(TAPS)], axis=0)
            h = w.astype(jnp.bfloat16)
            high.append(h)
            low.append((w - h.astype(jnp.float32)).astype(jnp.bfloat16))
        weights = jnp.concatenate(
            [jnp.concatenate(high, axis=1), jnp.concatenate(low, axis=1)], axis=0
        )
        acc_ref[...] = acc_ref[...] + lax.dot_general(
            weights, frames_ref[j], (((1,), (1,)), ((), ())), preferred_element_type=jnp.float32
        )
        return carry

    lax.fori_loop(0, steps, chunk, 0)
    g = acc_ref[: TAPS * ROWS] + acc_ref[TAPS * ROWS :]

    def term(t, f):
        return g[t * ROWS : (t + 1) * ROWS, f * HALF : (f + 1) * HALF]

    own, after = [], []
    for s in range(FRAMES):
        own.append(sum(term(f - s + 3, f) for f in range(s + 1)))
        if s < TAPS - 1:
            after.append(sum(term(f - 1 - s, f) for f in range(s + 1, FRAMES)))
    after.append(jnp.zeros_like(after[0]))
    own = jnp.concatenate(own, axis=1)
    after = jnp.concatenate(after, axis=1)
    for c in range(4):
        rows = slice(c * 8, (c + 1) * 8)
        piece = [part[rows, at : at + LANES] for part in (own, after) for at in (0, LANES)]
        piece = jnp.concatenate(piece, axis=0)
        place = Z_ORDER.index(c)
        for x in range(4):
            out_ref[place * 4 + x] = piece


def filterbank(voltages, taps, channels):
    steps = taps.shape[1] // CHUNK
    return pl.pallas_call(
        filterbank_kernel,
        in_specs=[
            pl.BlockSpec(memory_space=pltpu.SMEM),
            pl.BlockSpec(memory_space=pl.ANY),
            pl.BlockSpec(memory_space=pl.ANY),
        ],
        out_shape=jax.ShapeDtypeStruct((16, 32, LANES), jnp.float32),
        scratch_shapes=[
            pltpu.VMEM((steps, FRAMES * HALF, CHUNK), jnp.bfloat16),
            pltpu.VMEM((steps, TAPS, CHUNK), jnp.float32),
            pltpu.VMEM((ROWS, CHUNK), jnp.float32),
            pltpu.VMEM((ROWS, CHUNK), jnp.float32),
            pltpu.VMEM((2 * steps, ROWS, LANES), jnp.float32),
            pltpu.VMEM((2 * TAPS * ROWS, FRAMES * HALF), jnp.float32),
            pltpu.SemaphoreType.DMA((steps, FRAMES)),
            pltpu.SemaphoreType.DMA((steps,)),
        ],
        compiler_params=pltpu.CompilerParams(vmem_limit_bytes=VMEM_LIMIT),
        name="filterbank",
    )(channels, voltages, taps)


def arrange_kernel(got_ref, rows_ref):
    low = lax.broadcasted_iota(jnp.int32, (8, LANES), 1) < HALF

    def spectra(x, col, late):
        def part(x, at):
            place = Z_ORDER.index(col) * 4 + X_ORDER.index(x)
            return got_ref[place, pl.ds(at, 8)]

        total = part(x, 8 * late)
        if x > 0:
            total = total + part(x - 1, 16 + 8 * late)
        return total.astype(jnp.bfloat16).astype(jnp.float32)

    for x in range(4):
        first, second = [], []
        for late in range(2):
            a, b = [], []
            for pair in range(2):
                even = spectra(x, 2 * pair, late)
                odd = spectra(x, 2 * pair + 1, late)
                a.append(jnp.where(low, even, pltpu.roll(odd, HALF, 1)))
                b.append(jnp.where(low, pltpu.roll(even, HALF, 1), odd))
            first.append(jnp.concatenate(a, axis=1))
            second.append(jnp.concatenate(b, axis=1))
        block = jnp.concatenate(first + second, axis=0)
        rows_ref[32 * x : 32 * (x + 1)] = block.astype(jnp.bfloat16)


def arrange(got):
    return pl.pallas_call(
        arrange_kernel,
        out_shape=jax.ShapeDtypeStruct((LANES, 256), jnp.bfloat16),
        compiler_params=pltpu.CompilerParams(vmem_limit_bytes=SMALL_LIMIT),
        name="arrange",
    )(got)


def correlate_kernel(scale, rows_ref, near_ref, near_other_ref, far_ref, far_other_ref, out_ref, left_ref, right_ref, held_ref, sem):
    left = rows_ref[...].astype(jnp.float32)
    turned = [pltpu.roll(left[g * 8 : (g + 1) * 8], 4, 0) for g in range(LANES // 8)]
    turned = jnp.concatenate(turned, axis=0)
    depth = lax.broadcasted_iota(jnp.int32, turned.shape, 0)
    turned = jnp.where(depth // 4 % 2 == 0, turned, -turned)
    left_ref[0] = left.T
    left_ref[1] = turned.T
    width = near_ref.shape[1]
    mine = 2 * lax.axis_index("zl") + lax.axis_index("co")
    for k, block in enumerate((near_ref, near_other_ref, far_ref, far_other_ref)):
        column = pl.multiple_of((mine ^ k) * width, width)
        right_ref[:, pl.ds(column, width)] = block[...]

    lane = lax.broadcasted_iota(jnp.int32, left_ref.shape[1:], 1)

    def copy(k):
        return pltpu.make_async_copy(held_ref.at[k], out_ref.at[k // 2, k % 2], sem.at[k])

    for k in range(8):
        chosen = jnp.where(lane % 4 == k // 2, left_ref[k % 2], 0.0).astype(jnp.bfloat16)
        product = jnp.dot(chosen, right_ref[...], preferred_element_type=jnp.float32)
        held_ref[k] = (product * scale).astype(jnp.bfloat16)
        copy(k).start()
    for k in range(8):
        copy(k).wait()


def correlate(rows, blocks, scale):
    depth, width = rows.shape
    return pl.pallas_call(
        functools.partial(correlate_kernel, scale),
        in_specs=[pl.BlockSpec(memory_space=pltpu.VMEM)] * 5,
        out_specs=pl.BlockSpec(memory_space=pl.ANY),
        out_shape=jax.ShapeDtypeStruct((4, 2, width, 4 * width), jnp.bfloat16),
        scratch_shapes=[
            pltpu.VMEM((2, width, depth), jnp.float32),
            pltpu.VMEM((depth, 4 * width), jnp.bfloat16),
            pltpu.VMEM((8, width, 4 * width), jnp.bfloat16),
            pltpu.SemaphoreType.DMA((8,)),
        ],
        compiler_params=pltpu.CompilerParams(vmem_limit_bytes=SMALL_LIMIT),
        name="correlate",
    )(rows, *blocks)


def across_near():
    pairs = []
    for x in range(4):
        for y in range(4):
            source = (x + 2 - (y - x)) % 4
            pairs.append((source * 4 + x, x * 4 + y))
    return pairs


def across_far():
    pairs = []
    for x in range(4):
        for y in range(4):
            source = (x + 2 + (y - x)) % 4
            pairs.append((source * 4 + x, x * 4 + y))
    return pairs


def shards(voltages, taps, channels):
    pieces = filterbank(voltages, taps, channels)
    got = lax.all_to_all(pieces, AXES, 0, 0, axis_index_groups=exchange_groups(), tiled=True)
    rows = arrange(got)
    swap = [(0, 1), (1, 0)]
    pairs = [(2 * s + z, 2 * d + 1 - z) for s, d in across_far() for z in range(2)]
    near = lax.ppermute(rows, ("x", "y"), across_near())
    far = lax.ppermute(rows, ("x", "y", "zl"), pairs)
    near_other = lax.ppermute(near, "co", swap)
    far_other = lax.ppermute(far, "co", swap)
    return correlate(rows, (near, near_other, far, far_other), 1.0 / 16.0)


def solution(mesh):
    fine = Mesh(mesh.devices.reshape(4, 4, 4, 2, 2), ("x", "zh", "y", "zl", "co"))
    placed = (P(("y", "zl", "co", "zh"), "x"), P(), P())
    return jax.shard_map(
        shards,
        mesh=fine,
        in_specs=placed,
        out_specs=P("zh", None, ("y", "zl", "co"), "x"),
        check_vma=False,
    )
```
